32 devices in a mesh: clips: 2 (over y), tile: 4 (over x, core), tm: 4 (over z).
Axes of the slice: x: 2, y: 2, z: 4, core: 2. Of those that a mesh axis runs over, the one named last changes fastest.
Arguments:
- frames: bfloat16 [8, 120, 32, 128], P(('clips', 'tm'), None, 'tile'), parts along dimension 0, may hold values from -6 to 6
- ln_gain: float32 [2, 2, 120], replicated, may hold values from 0.5 to 1.5
- qkv_weight: bfloat16 [2, 120, 360], replicated, may hold values from -4 to 4
- out_weight: bfloat16 [2, 120, 120], replicated, may hold values from -0.5 to 0.5
- gate_weight: bfloat16 [2, 120, 240], replicated, may hold values from -0.5 to 0.5
- up_weight: bfloat16 [2, 120, 240], replicated, may hold values from -0.5 to 0.5
- down_weight: bfloat16 [2, 240, 120], replicated, may hold values from -0.375 to 0.375
- conv_weight: bfloat16 [2, 9, 120, 120], replicated, may hold values from -0.1875 to 0.1875
- conv_bias: float32 [2, 120], replicated, may hold values from -3 to 3
Outputs:
- restored: bfloat16 [8, 120, 32, 128], P(('clips', 'tm'), None, 'tile'), parts along dimension 0
The draws below stay inside these ranges and needn't reach their ends.
There are 2 independent parts, one for each index of `clips`. The reference program is written for one: setup_inputs(seed, part) draws one part's arguments, and reference() takes and returns one part's arrays. A program takes and returns all parts, laid end to end along the dimension named above; an argument that names none is the same for every part. Nothing has to cross between parts.
All inputs are finite; a program needn't handle non-finite values.
Results may differ from the reference program's by a relative error of at most 0.0084.
Values may be sent and summed in bfloat16 or wider, within the bound.
A program may use at most 64 MiB of HBM per device.

```python
import jax
import jax.numpy as jnp
from jax import lax

HEADS = 6
HD = 20
C = 120
FF = 240
LAYERS = 2
W = 128
FRAMES = 4
H = 32


def draw_qkv_weight(key, part):
    base = jax.random.normal(key, (LAYERS, C, 3 * C), jnp.float32) * C ** (-0.5)
    return jnp.clip(base, -4.0, 4.0).astype(jnp.bfloat16)


def shard_levels(key, extent, cuts, smallest, largest):
    loudness = 1.0
    for axis_at, shards_of in cuts:
        draws = jax.random.uniform(jax.random.fold_in(jax.random.fold_in(key, 6), axis_at), (shards_of,), jnp.float32, smallest / len(cuts), largest / len(cuts))
        loudness = loudness * jnp.repeat(jnp.exp(draws), extent[axis_at] // shards_of).reshape((-1,) + (1,) * (len(extent) - 1 - axis_at))
    return loudness


def bell_draw(key, shape, width, limit, cuts=(), kind=jnp.bfloat16):
    factor_of = shard_levels(key, shape, cuts, -0.22, 0.18) if cuts else 1.0
    array = jax.random.normal(key, shape, jnp.float32) * width * factor_of
    return jnp.minimum(jnp.maximum(array, -limit), limit).astype(kind)


def setup_inputs(seed: int = 0, part: int = 0) -> dict:
    key_list = jax.random.split(jax.random.key(seed), 10)
    part_keys = jax.random.split(jax.random.fold_in(key_list[9], part), 10)
    frames = bell_draw(part_keys[0], (FRAMES, C, H, W), 1.0, 6.0, ((0, 4), (2, 4)))
    ln_gain = jnp.clip(jax.random.uniform(key_list[1], (LAYERS, 2, C), jnp.float32, 0.5, 1.5), 0.5, 1.5)
    qkv_weight = draw_qkv_weight(jax.random.fold_in(key_list[9], 71), part)
    out_weight = bell_draw(key_list[3], (LAYERS, C, C), C ** -0.5, 0.5)
    gate_weight = bell_draw(key_list[4], (LAYERS, C, FF), C ** -0.5, 0.5)
    up_weight = bell_draw(key_list[5], (LAYERS, C, FF), C ** -0.5, 0.5)
    down_weight = bell_draw(key_list[6], (LAYERS, FF, C), FF ** -0.5, 0.375)
    conv_weight = bell_draw(key_list[7], (LAYERS, 9, C, C), (9 * C) ** -0.5, 0.1875)
    conv_bias = bell_draw(key_list[8], (LAYERS, C), 0.5, 3.0, (), jnp.float32)
    return {"frames": frames, "ln_gain": ln_gain, "qkv_weight": qkv_weight, "out_weight": out_weight, "gate_weight": gate_weight, "up_weight": up_weight, "down_weight": down_weight, "conv_weight": conv_weight, "conv_bias": conv_bias}


def layer_norm(tensor, gain):
    center = tensor - lax.optimization_barrier(jnp.mean(tensor, axis=-3, keepdims=True))
    spread = lax.optimization_barrier(jnp.mean(center * center, axis=-3, keepdims=True))
    return (center * lax.rsqrt(spread + 1e-05) * gain[:, None, None]).astype(jnp.bfloat16)

def to_windows(tensor):
    row_count, col_count = (tensor.shape[1], tensor.shape[2])
    split = tensor.reshape(HEADS, HD, row_count // 8, 8, col_count // 8, 8)
    return split.transpose(0, 2, 4, 3, 5, 1).reshape(HEADS, row_count // 8 * (col_count // 8), 64, HD)

def from_windows(tensor, row_count, col_count):
    split = tensor.reshape(HEADS, row_count // 8, col_count // 8, 8, 8, HD)
    return split.transpose(0, 5, 1, 3, 2, 4).reshape(HEADS * HD, row_count, col_count)

def attention(queries, own_keys, own_values, far_keys, far_values):
    row_count, col_count = (queries.shape[1], queries.shape[2])
    q_windows = to_windows(queries).astype(jnp.float32)
    all_keys = jnp.concatenate([to_windows(own_keys), to_windows(far_keys)], axis=2).astype(jnp.float32)
    all_values = jnp.concatenate([to_windows(own_values), to_windows(far_values)], axis=2).astype(jnp.float32)
    scores = jnp.einsum('hnqd,hnkd->hnqk', q_windows, all_keys) * HD ** (-0.5)
    weights = lax.optimization_barrier(jax.nn.softmax(scores, axis=-1).astype(jnp.bfloat16)).astype(jnp.float32)
    result = jnp.einsum('hnqk,hnkd->hnqd', weights, all_values)
    return from_windows(result, row_count, col_count).astype(jnp.bfloat16)

def project(tensor, weight):
    return jnp.einsum('crw,cd->drw', tensor.astype(jnp.float32), weight.astype(jnp.float32))

def reference(frames, ln_gain, qkv_weight, out_weight, gate_weight, up_weight, down_weight, conv_weight, conv_bias):
    stream = frames.astype(jnp.float32)
    frame_ids = jnp.arange(FRAMES, dtype=jnp.int32)
    for layer_index in range(LAYERS):
        shifted = layer_index % 2 == 1
        normed = layer_norm(stream, ln_gain[layer_index, 0])
        if shifted:
            window_input = jnp.roll(normed, (-4, -4), axis=(2, 3))
        else:
            window_input = normed
        packed = lax.map(lambda one_frame: project(one_frame, qkv_weight[layer_index]).astype(jnp.bfloat16), window_input)
        queries = packed[:, :C]
        key_all = packed[:, C:2 * C]
        value_all = packed[:, 2 * C:]
        if shifted:
            partner = jnp.where(frame_ids % 2 == 1, (frame_ids + 1) % FRAMES, (frame_ids - 1) % FRAMES).astype(jnp.int32)
        else:
            partner = jnp.bitwise_xor(frame_ids, 1).astype(jnp.int32)
        mixed = lax.map(lambda group: attention(*group), (queries, key_all, value_all, key_all[partner], value_all[partner]))
        if shifted:
            unrolled = jnp.roll(mixed, (4, 4), axis=(2, 3))
        else:
            unrolled = mixed
        attended = stream + lax.map(lambda one_frame: project(one_frame, out_weight[layer_index]), unrolled)
        normed_ff = layer_norm(attended, ln_gain[layer_index, 1])

        def feed(one_frame):
            gate_part = project(one_frame, gate_weight[layer_index])
            up_part = project(one_frame, up_weight[layer_index])
            hidden = (jax.nn.gelu(gate_part, approximate=False) * up_part).astype(jnp.bfloat16)
            return project(hidden, down_weight[layer_index])
        fed = attended + lax.map(feed, normed_ff)
        rounded = fed.astype(jnp.bfloat16)

        def convolve(one_frame):
            padded = jnp.pad(one_frame, ((0, 0), (1, 1), (1, 1)))
            row_count, col_count = (one_frame.shape[1], one_frame.shape[2])
            total = jnp.zeros((C, row_count, col_count), jnp.float32)
            for tap_row in range(3):
                for tap_col in range(3):
                    window = padded[:, tap_row:tap_row + row_count, tap_col:tap_col + col_count]
                    total = total + project(window, conv_weight[layer_index, 3 * tap_row + tap_col])
            return total
        stream = fed + lax.map(convolve, rounded) + conv_bias[layer_index][None, :, None, None]
    return stream.astype(jnp.bfloat16)
```

```python
import functools

import jax
import jax.numpy as jnp
from jax import lax
from jax.experimental import pallas as pl
from jax.experimental.pallas import tpu as pltpu
from jax.sharding import PartitionSpec as P

HEADS = 6
HD = 20
LAYERS = 2
LANES = 128
WIN = 8
HALF = WIN // 2
GROUP = 4
F32 = jnp.float32
BF16 = jnp.bfloat16
MESH = pl.DeviceIdType.MESH


def dot(a, b):
    return lax.dot_general(a, b, (((1,), (0,)), ((), ())), preferred_element_type=F32)


def dot_nt(a, b):
    return lax.dot_general(a, b, (((1,), (1,)), ((), ())), preferred_element_type=F32)


def lanes_of(shape):
    return lax.broadcasted_iota(jnp.int32, shape, len(shape) - 1)


def layer_norm(x, gain, channels):
    mean = jnp.sum(x, axis=-1, keepdims=True) * (1.0 / channels)
    center = jnp.where(lanes_of(x.shape) < channels, x - mean, 0.0)
    spread = jnp.sum(center * center, axis=-1, keepdims=True) * (1.0 / channels)
    return center * lax.rsqrt(spread + 1e-05) * gain


def kernel(
    frames, ln_gain, qkv_w, out_w, gate_w, up_w, down_w, conv_w, conv_b, out,
    xs, stream, kv0, kv1, bsend, ret, mix0, mix1, yp0, yp1,
    pq, po, pgu, pd, pc, tmp, small,
    send0, recv0, send1, recv1, send_ret, recv_ret, send_halo, recv_halo,
):
    channels, rows, cols = frames.shape[1:]
    hidden = gate_w.shape[2]
    windows = cols // WIN
    groups = windows // GROUP
    tiles, count = lax.axis_size("tile"), lax.axis_size("tm")
    t, f = lax.axis_index("tile"), lax.axis_index("tm")
    odd = lax.rem(f, 2)
    even_pair = f + 1 - 2 * odd
    odd_pair = lax.rem(f + 2 * odd - 1 + count, count)
    above, below = lax.rem(t + tiles - 1, tiles), lax.rem(t + 1, tiles)

    barrier = pltpu.get_barrier_semaphore()
    peers = [
        {"tm": even_pair}, {"tm": odd_pair}, {"tile": above}, {"tile": below},
        {"tile": above, "tm": odd_pair}, {"tile": below, "tm": odd_pair},
    ]
    for peer in peers:
        pl.semaphore_signal(barrier, inc=1, device_id=peer, device_id_type=MESH)

    def remote(src, dst, send, recv, peer):
        return pltpu.make_async_remote_copy(
            src_ref=src, dst_ref=dst, send_sem=send, recv_sem=recv,
            device_id=peer, device_id_type=MESH,
        )

    def pair_copy(g):
        at = pl.ds(g * GROUP, GROUP)
        return remote(
            kv0.at[at, pl.ds(0, 64)], kv0.at[at, pl.ds(64, 64)],
            send0.at[g], recv0.at[g], {"tm": even_pair},
        )

    def odd_copies(g):
        at = pl.ds(g * GROUP, GROUP)
        return [
            remote(kv1.at[at, pl.ds(0, 32)], kv1.at[at, pl.ds(64, 32)],
                   send1.at[0, g], recv1.at[0, g], {"tm": odd_pair}),
            remote(bsend.at[at], kv1.at[at, pl.ds(96, 32)],
                   send1.at[1, g], recv1.at[1, g], {"tile": above, "tm": odd_pair}),
            remote(bsend.at[at], kv1.at[at, pl.ds(32, 32)],
                   send1.at[2, g], recv1.at[2, g], {"tile": above}),
        ]

    def ret_copy(g):
        at = pl.ds(g * GROUP, GROUP)
        return remote(ret.at[at], mix1.at[0, at], send_ret.at[g], recv_ret.at[g], {"tile": below})

    def halo_copy(layer, side):
        yp = (yp0, yp1)[layer]
        if side == 0:
            src, dst, peer = yp.at[1], yp.at[rows + 1], {"tile": above}
        else:
            src, dst, peer = yp.at[rows], yp.at[0], {"tile": below}
        return remote(src, dst, send_halo.at[layer, side], recv_halo.at[layer, side], peer)

    small[...] = jnp.zeros_like(small)
    for layer in range(LAYERS):
        small[2 * layer : 2 * layer + 2, 0:channels] = ln_gain[layer]
    small[4 : 4 + LAYERS, 0:channels] = conv_b[...]

    xs[...] = frames[0].astype(F32).reshape(channels * rows, cols)
    for r in range(rows):
        row = xs[pl.ds(r, channels, stride=rows), :]
        row = jnp.concatenate([row, jnp.zeros((LANES - channels, cols), F32)], axis=0)
        stream[r // HALF, :, r % HALF] = row.T.reshape(windows, WIN, LANES)

    for g in range(groups):
        at = pl.ds(g * GROUP, GROUP)
        for half in range(2):
            x = stream[half, at].reshape(GROUP * 32, LANES)
            normed = layer_norm(x, small[0:1, :], channels)
            kv0[at, pl.ds(32 * half, 32)] = normed.astype(BF16).reshape(GROUP, 32, LANES)
        if g == 0:
            pl.semaphore_wait(barrier, len(peers))
        pair_copy(g).start()

    tmp[...] = jnp.zeros_like(tmp)
    for layer in range(LAYERS):
        tmp[0:channels, 0 : 3 * channels] = qkv_w[layer].astype(F32)
        whole = tmp[0:LANES, 0:384]
        for j in range(3):
            part = whole if j == 0 else pltpu.roll(whole, 384 - channels * j, 1)
            part = part[:, 0:LANES]
            part = jnp.where(lanes_of(part.shape) < channels, part, 0.0)
            pq[layer, :, LANES * j : LANES * (j + 1)] = part.astype(BF16)
        tmp[0:LANES, 0:384] = jnp.zeros((LANES, 384), F32)
        for j, weight in enumerate((gate_w, up_w)):
            tmp[0:channels, 0:hidden] = weight[layer].astype(F32)
            pgu[layer, :, 256 * j : 256 * (j + 1)] = tmp[0:LANES, 0:256].astype(BF16)
        tmp[0:LANES, 0:256] = jnp.zeros((LANES, 256), F32)
        tmp[0:channels, 0:channels] = out_w[layer].astype(F32)
        po[layer] = tmp[0:LANES, 0:LANES].astype(BF16)
        for a in range(3):
            for b in range(3):
                tmp[0:channels, 0:channels] = conv_w[layer, 3 * a + b].astype(F32)
                pc[layer, LANES * a : LANES * (a + 1), LANES * b : LANES * (b + 1)] = tmp[
                    0:LANES, 0:LANES
                ].astype(BF16)
        tmp[0:hidden, 0:channels] = down_w[layer].astype(F32)
        pd[layer] = tmp[0:256, 0:LANES].astype(BF16)
        tmp[0:256, 0:LANES] = jnp.zeros((256, LANES), F32)

    scale = HD ** (-0.5) * 1.4426950408889634

    def attend(layer, kv, g, put):
        at = pl.ds(g * GROUP, GROUP)
        all_in = kv[at].reshape(GROUP * 128, LANES)
        q_in = kv[at, pl.ds(0, 64)].reshape(GROUP * 64, LANES)
        packed = dot(all_in, pq[layer, :, LANES:384]).astype(BF16)
        queries = dot(q_in, pq[layer, :, 0:LANES]).astype(BF16).astype(F32)
        lane = lanes_of((64, LANES))
        head = [(lane >= HD * h) & (lane < HD * (h + 1)) for h in range(HEADS)]
        ones = jnp.ones((128, LANES), BF16)
        for i in range(GROUP):
            q = queries[64 * i : 64 * (i + 1)]
            q = jnp.concatenate([jnp.where(head[h], q, 0.0).astype(BF16) for h in range(HEADS)], axis=0)
            k = packed[128 * i : 128 * (i + 1), 0:LANES]
            v = jnp.concatenate([packed[128 * i : 128 * (i + 1), LANES:256], ones], axis=1)
            scores = dot_nt(q, k)
            top = jnp.max(scores, axis=-1, keepdims=True)
            weights = jnp.exp2((scores - top) * scale).astype(BF16)
            both = dot(weights, v)
            mixed, total = both[0:64, 0:LANES], both[0:64, LANES:256]
            for h in range(1, HEADS):
                mixed = jnp.where(head[h], both[64 * h : 64 * (h + 1), 0:LANES], mixed)
                total = jnp.where(head[h], both[64 * h : 64 * (h + 1), LANES:256], total)
            mixed = (mixed / total).astype(BF16)
            put(g * GROUP + i, mixed)

    def feed(layer, mix, half):
        piece = 8
        yp = (yp0, yp1)[layer]
        for p in range(windows // piece):
            at = pl.ds(piece * p, piece)
            x = stream[half, at].reshape(piece * 32, LANES)
            x = x + dot(mix[half, at].reshape(piece * 32, LANES), po[layer])
            normed = layer_norm(x, small[2 * layer + 1 : 2 * layer + 2, :], channels).astype(BF16)
            gate = dot(normed, pgu[layer, :, 0:256])
            up = dot(normed, pgu[layer, :, 256:512])
            act = 0.5 * gate * (1.0 + lax.erf(gate * 0.7071067811865476)) * up
            x = x + dot(act.astype(BF16), pd[layer])
            stream[half, at] = x.reshape(piece, HALF, WIN, LANES)
        for i in range(HALF):
            yp[1 + HALF * half + i] = stream[half, :, i].reshape(cols, LANES).astype(BF16)

    def convolve(layer, r, first_col, last_col):
        yp = (yp0, yp1)[layer]
        parts = [yp[r], yp[r + 1], yp[r + 2]]
        if r == 0:
            parts[0] = jnp.where(t == 0, jnp.zeros_like(parts[0]), parts[0])
        if r == rows - 1:
            parts[2] = jnp.where(t == tiles - 1, jnp.zeros_like(parts[2]), parts[2])
        taps = dot(jnp.concatenate(parts, axis=1), pc[layer])
        at = lax.broadcasted_iota(jnp.int32, (cols, LANES), 0)
        total = taps[:, LANES : 2 * LANES]
        total += jnp.where(at == first_col, 0.0, pltpu.roll(taps[:, 0:LANES], 1, 0))
        total += jnp.where(at == last_col, 0.0, pltpu.roll(taps[:, 2 * LANES :], cols - 1, 0))
        fed = stream[r // HALF, :, r % HALF].reshape(cols, LANES)
        return fed + (total + small[4 + layer : 5 + layer, :])

    inner = list(range(1, rows - 1))

    def put0(n, mixed):
        mix0[0, n] = mixed[0:32]
        mix0[1, n] = mixed[32:64]

    def step0(g, carry):
        pair_copy(g).wait_recv()
        attend(0, kv0, g, put0)
        return carry

    lax.fori_loop(0, groups, step0, 0)
    for half in range(2):
        feed(0, mix0, half)
        halo_copy(0, half).start()

    def finish0(r):
        row = pltpu.roll(convolve(0, r, 0, cols - 1), cols - HALF, 0)
        stream[r // HALF, :, r % HALF] = row.reshape(windows, WIN, LANES)

    for r in inner:
        finish0(r)
    for side in range(2):
        halo_copy(0, side).wait_recv()
    finish0(0)
    finish0(rows - 1)

    for g in range(groups):
        at = pl.ds(g * GROUP, GROUP)
        for half in range(2):
            x = stream[half, at].reshape(GROUP * 32, LANES)
            normed = layer_norm(x, small[2:3, :], channels).astype(BF16).reshape(GROUP, 32, LANES)
            if half == 0:
                bsend[at] = normed
            else:
                kv1[at, pl.ds(0, 32)] = normed
        for copy in odd_copies(g):
            copy.start()

    def put1(n, mixed):
        mix1[1, n] = mixed[0:32]
        ret[n] = mixed[32:64]

    def step1(g, carry):
        for copy in odd_copies(g):
            copy.wait_recv()
        attend(1, kv1, g, put1)
        ret_copy(g).start()
        return carry

    lax.fori_loop(0, groups, step1, 0)
    feed(1, mix1, 1)
    halo_copy(1, 1).start()
    for g in range(groups):
        ret_copy(g).wait_recv()
    feed(1, mix1, 0)
    halo_copy(1, 0).start()

    def finish1(r):
        row = convolve(1, r, cols - HALF, cols - HALF - 1)
        row = pltpu.roll(row.T, HALF, 1)
        xs[pl.ds(r, channels, stride=rows), :] = row[0:channels]

    for r in inner:
        finish1(r)
    for side in range(2):
        halo_copy(1, side).wait_recv()
    finish1(0)
    finish1(rows - 1)
    out[0] = xs[...].reshape(channels, rows, cols).astype(BF16)

    for g in range(groups):
        pair_copy(g).wait_send()
        for copy in odd_copies(g):
            copy.wait_send()
        ret_copy(g).wait_send()
    for layer in range(LAYERS):
        for side in range(2):
            halo_copy(layer, side).wait_send()


def on_device(*args):
    frames = args[0]
    _, channels, rows, cols = frames.shape
    windows = cols // WIN
    groups = windows // GROUP
    dma = pltpu.SemaphoreType.DMA
    vmem = pl.BlockSpec(memory_space=pltpu.VMEM)
    return pl.pallas_call(
        kernel,
        out_shape=jax.ShapeDtypeStruct(frames.shape, BF16),
        in_specs=[vmem] * len(args),
        out_specs=vmem,
        scratch_shapes=[
            pltpu.VMEM((channels * rows, cols), F32),
            pltpu.VMEM((2, windows, HALF, WIN, LANES), F32),
            pltpu.VMEM((windows, 128, LANES), BF16),
            pltpu.VMEM((windows, 128, LANES), BF16),
            pltpu.VMEM((windows, 32, LANES), BF16),
            pltpu.VMEM((windows, 32, LANES), BF16),
            pltpu.VMEM((2, windows, 32, LANES), BF16),
            pltpu.VMEM((2, windows, 32, LANES), BF16),
            pltpu.VMEM((rows + 2, cols, LANES), BF16),
            pltpu.VMEM((rows + 2, cols, LANES), BF16),
            pltpu.VMEM((LAYERS, LANES, 384), BF16),
            pltpu.VMEM((LAYERS, LANES, LANES), BF16),
            pltpu.VMEM((LAYERS, LANES, 512), BF16),
            pltpu.VMEM((LAYERS, 256, LANES), BF16),
            pltpu.VMEM((LAYERS, 384, 384), BF16),
            pltpu.VMEM((256, 384), F32),
            pltpu.VMEM((8, LANES), F32),
            dma((groups,)), dma((groups,)),
            dma((3, groups)), dma((3, groups)),
            dma((groups,)), dma((groups,)),
            dma((LAYERS, 2)), dma((LAYERS, 2)),
        ],
        compiler_params=pltpu.CompilerParams(
            collective_id=0, has_side_effects=True, vmem_limit_bytes=40 * 2**20
        ),
    )(*args)


def solution(mesh):
    in_specs = (P(("clips", "tm"), None, "tile", None), P(), P(), P(), P(), P(), P(), P(), P())
    out_specs = P(("clips", "tm"), None, "tile", None)
    return jax.shard_map(
        on_device, mesh=mesh, in_specs=in_specs, out_specs=out_specs, check_vma=False
    )
```

```python
import functools

import jax
import jax.numpy as jnp
from jax import lax
from jax.experimental import pallas as pl
from jax.experimental.pallas import tpu as pltpu
from jax.sharding import PartitionSpec as P

HEADS = 6
HD = 20
LAYERS = 2
LANES = 128
WIN = 8
HALF = WIN // 2
GROUP = 4
F32 = jnp.float32
BF16 = jnp.bfloat16
MESH = pl.DeviceIdType.MESH


def dot(a, b):
    return lax.dot_general(a, b, (((1,), (0,)), ((), ())), preferred_element_type=F32)


def dot_nt(a, b):
    return lax.dot_general(a, b, (((1,), (1,)), ((), ())), preferred_element_type=F32)


def lanes_of(shape):
    return lax.broadcasted_iota(jnp.int32, shape, len(shape) - 1)


def layer_norm(x, gain, channels):
    mean = jnp.sum(x, axis=-1, keepdims=True) * (1.0 / channels)
    center = jnp.where(lanes_of(x.shape) < channels, x - mean, 0.0)
    spread = jnp.sum(center * center, axis=-1, keepdims=True) * (1.0 / channels)
    return center * lax.rsqrt(spread + 1e-05) * gain


def kernel(
    frames_h, ln_gain_h, qkv_h, out_h, gate_h, up_h, down_h, conv_h, conv_b_h, out,
    frames, ln_gain, qkv_w, out_w, gate_w, up_w, down_w, conv_w, conv_b, load_sem,
    xs, stream, fedn, taps, kv0, kv1, bsend, ret, mix0, mix1, yp0, yp1,
    pq, po, pgu, pd, pc, tmp, small,
    send0, recv0, send1, recv1, send_ret, recv_ret, send_halo, recv_halo,
):
    channels, rows, cols = frames.shape[1:]
    hidden = gate_w.shape[2]
    windows = cols // WIN
    groups = windows // GROUP
    span = GROUP * WIN
    tiles, count = lax.axis_size("tile"), lax.axis_size("tm")
    t, f = lax.axis_index("tile"), lax.axis_index("tm")
    odd = lax.rem(f, 2)
    even_pair = f + 1 - 2 * odd
    odd_pair = lax.rem(f + 2 * odd - 1 + count, count)
    above, below = lax.rem(t + tiles - 1, tiles), lax.rem(t + 1, tiles)

    pairs = [
        (frames_h, frames), (ln_gain_h, ln_gain), (conv_b_h, conv_b), (qkv_h, qkv_w), (out_h, out_w),
        (gate_h, gate_w), (up_h, up_w), (down_h, down_w), (conv_h, conv_w),
    ]
    loads = [pltpu.make_async_copy(a, b, load_sem.at[i]) for i, (a, b) in enumerate(pairs)]
    for load in loads:
        load.start()
    barrier = pltpu.get_barrier_semaphore()
    peers = [
        {"tm": even_pair}, {"tm": odd_pair}, {"tile": above}, {"tile": below},
        {"tile": above, "tm": odd_pair}, {"tile": below, "tm": odd_pair},
    ]
    for peer in peers:
        pl.semaphore_signal(barrier, inc=1, device_id=peer, device_id_type=MESH)

    def remote(src, dst, send, recv, peer):
        return pltpu.make_async_remote_copy(
            src_ref=src, dst_ref=dst, send_sem=send, recv_sem=recv,
            device_id=peer, device_id_type=MESH,
        )

    def pair_copy(g):
        at = pl.ds(g * GROUP, GROUP)
        return remote(
            kv0.at[at, pl.ds(0, 64)], kv0.at[at, pl.ds(64, 64)],
            send0.at[g], recv0.at[g], {"tm": even_pair},
        )

    def odd_copies(g):
        at = pl.ds(g * GROUP, GROUP)
        return [
            remote(kv1.at[at, pl.ds(0, 32)], kv1.at[at, pl.ds(64, 32)],
                   send1.at[0, g], recv1.at[0, g], {"tm": odd_pair}),
            remote(bsend.at[at], kv1.at[at, pl.ds(96, 32)],
                   send1.at[1, g], recv1.at[1, g], {"tile": above, "tm": odd_pair}),
            remote(bsend.at[at], kv1.at[at, pl.ds(32, 32)],
                   send1.at[2, g], recv1.at[2, g], {"tile": above}),
        ]

    def ret_copy(g):
        at = pl.ds(g * GROUP, GROUP)
        return remote(ret.at[at], mix1.at[0, at], send_ret.at[g], recv_ret.at[g], {"tile": below})

    def halo_copy(layer, side, g=0):
        yp = (yp0, yp1)[layer]
        at = pl.ds(g * span, span) if layer == 0 else pl.ds(0, cols)
        slot = g if layer == 0 else groups
        if side == 0:
            src, dst, peer = yp.at[1, at], yp.at[rows + 1, at], {"tile": above}
        else:
            src, dst, peer = yp.at[rows, at], yp.at[0, at], {"tile": below}
        return remote(src, dst, send_halo.at[slot, side], recv_halo.at[slot, side], peer)

    for load in loads[0:3]:
        load.wait()
    small[...] = jnp.zeros_like(small)
    for layer in range(LAYERS):
        small[2 * layer : 2 * layer + 2, 0:channels] = ln_gain[layer]
    small[4 : 4 + LAYERS, 0:channels] = conv_b[...]

    xs[...] = frames[0].astype(F32).reshape(channels * rows, cols)
    for r in range(rows):
        row = xs[pl.ds(r, channels, stride=rows), :]
        row = jnp.concatenate([row, jnp.zeros((LANES - channels, cols), F32)], axis=0)
        stream[r // HALF, :, r % HALF] = row.T.reshape(windows, WIN, LANES)

    for g in range(groups):
        at = pl.ds(g * GROUP, GROUP)
        for half in range(2):
            x = stream[half, at].reshape(GROUP * 32, LANES)
            normed = layer_norm(x, small[0:1, :], channels)
            kv0[at, pl.ds(32 * half, 32)] = normed.astype(BF16).reshape(GROUP, 32, LANES)
        if g == 0:
            pl.semaphore_wait(barrier, len(peers))
        pair_copy(g).start()

    for load in loads[3:]:
        load.wait()
    tmp[...] = jnp.zeros_like(tmp)

    def pad_weights(layer):
        tmp[0:channels, 0 : 3 * channels] = qkv_w[layer].astype(F32)
        whole = tmp[0:LANES, 0:384]
        for j in range(3):
            part = whole if j == 0 else pltpu.roll(whole, 384 - channels * j, 1)
            part = part[:, 0:LANES]
            part = jnp.where(lanes_of(part.shape) < channels, part, 0.0)
            pq[layer, :, LANES * j : LANES * (j + 1)] = part.astype(BF16)
        tmp[0:LANES, 0:384] = jnp.zeros((LANES, 384), F32)
        for j, weight in enumerate((gate_w, up_w)):
            tmp[0:channels, 0:hidden] = weight[layer].astype(F32)
            pgu[layer, :, 256 * j : 256 * (j + 1)] = tmp[0:LANES, 0:256].astype(BF16)
        tmp[0:LANES, 0:256] = jnp.zeros((LANES, 256), F32)
        tmp[0:channels, 0:channels] = out_w[layer].astype(F32)
        po[layer] = tmp[0:LANES, 0:LANES].astype(BF16)
        for a in range(3):
            for b in range(3):
                tmp[0:channels, 0:channels] = conv_w[layer, 3 * a + b].astype(F32)
                pc[layer, LANES * a : LANES * (a + 1), LANES * b : LANES * (b + 1)] = tmp[
                    0:LANES, 0:LANES
                ].astype(BF16)
        tmp[0:hidden, 0:channels] = down_w[layer].astype(F32)
        pd[layer] = tmp[0:256, 0:LANES].astype(BF16)
        tmp[0:256, 0:LANES] = jnp.zeros((256, LANES), F32)

    pad_weights(0)

    scale = HD ** (-0.5) * 1.4426950408889634

    def attend(layer, kv, g, put):
        at = pl.ds(g * GROUP, GROUP)
        all_in = kv[at].reshape(GROUP * 128, LANES)
        q_in = kv[at, pl.ds(0, 64)].reshape(GROUP * 64, LANES)
        packed = dot(all_in, pq[layer, :, LANES:384]).astype(BF16)
        queries = dot(q_in, pq[layer, :, 0:LANES]).astype(BF16).astype(F32)
        lane = lanes_of((64, LANES))
        head = [(lane >= HD * h) & (lane < HD * (h + 1)) for h in range(HEADS)]
        ones = jnp.ones((128, LANES), BF16)
        for i in range(GROUP):
            q = queries[64 * i : 64 * (i + 1)]
            q = jnp.concatenate([jnp.where(head[h], q, 0.0).astype(BF16) for h in range(HEADS)], axis=0)
            k = packed[128 * i : 128 * (i + 1), 0:LANES]
            v = jnp.concatenate([packed[128 * i : 128 * (i + 1), LANES:256], ones], axis=1)
            scores = dot_nt(q, k)
            top = jnp.max(scores, axis=-1, keepdims=True)
            weights = jnp.exp2((scores - top) * scale).astype(BF16)
            both = dot(weights, v)
            mixed, total = both[0:64, 0:LANES], both[0:64, LANES:256]
            for h in range(1, HEADS):
                mixed = jnp.where(head[h], both[64 * h : 64 * (h + 1), 0:LANES], mixed)
                total = jnp.where(head[h], both[64 * h : 64 * (h + 1), LANES:256], total)
            mixed = (mixed / total).astype(BF16)
            put(g * GROUP + i, mixed)

    def feed(layer, mix, half, g):
        at = pl.ds(g * GROUP, GROUP)
        x = stream[half, at].reshape(GROUP * 32, LANES)
        x = x + dot(mix[half, at].reshape(GROUP * 32, LANES), po[layer])
        normed = layer_norm(x, small[2 * layer + 1 : 2 * layer + 2, :], channels).astype(BF16)
        gate = dot(normed, pgu[layer, :, 0:256])
        up = dot(normed, pgu[layer, :, 256:512])
        act = 0.5 * gate * (1.0 + lax.erf(gate * 0.7071067811865476)) * up
        x = x + dot(act.astype(BF16), pd[layer])
        stream[half, at] = x.reshape(GROUP, HALF, WIN, LANES)
        for i in range(HALF):
            row = stream[half, at, i].reshape(span, LANES)
            (yp0, yp1)[layer][1 + HALF * half + i, pl.ds(g * span, span)] = row.astype(BF16)
            if layer == 0:
                fedn[HALF * half + i, g * span : (g + 1) * span] = row

    def multiply0(g):
        at = pl.ds(g * span, span)
        lines = [yp0[r, at] for r in range(rows + 2)]
        lines[0] = jnp.where(t == 0, jnp.zeros_like(lines[0]), lines[0])
        lines[-1] = jnp.where(t == tiles - 1, jnp.zeros_like(lines[-1]), lines[-1])
        lhs = [jnp.concatenate(lines[r : r + 3], axis=1) for r in range(rows)]
        result = dot(jnp.concatenate(lhs, axis=0), pc[0])
        for r in range(rows):
            taps[r, g * span : (g + 1) * span] = result[span * r : span * (r + 1)]
            if g == 0:
                taps[r, cols : cols + 8] = result[span * r : span * r + 8]
                fedn[r, cols : cols + 8] = fedn[r, 0:8]

    def add0(g):
        start = g * span + HALF
        at = g * span + lax.broadcasted_iota(jnp.int32, (span, LANES), 0)
        for r in range(rows):
            left = taps[r, start - 1 : start - 1 + span, 0:LANES]
            mid = taps[r, start : start + span, LANES : 2 * LANES]
            right = taps[r, start + 1 : start + 1 + span, 2 * LANES : 3 * LANES]
            left = jnp.where(at == cols - HALF, 0.0, left)
            right = jnp.where(at == cols - HALF - 1, 0.0, right)
            row = fedn[r, start : start + span] + (left + mid + right + small[4:5, :])
            stream[r // HALF, pl.ds(g * GROUP, GROUP), r % HALF] = row.reshape(GROUP, WIN, LANES)

    def convolve(layer, r, first_col, last_col):
        yp = (yp0, yp1)[layer]
        parts = [yp[r], yp[r + 1], yp[r + 2]]
        if r == 0:
            parts[0] = jnp.where(t == 0, jnp.zeros_like(parts[0]), parts[0])
        if r == rows - 1:
            parts[2] = jnp.where(t == tiles - 1, jnp.zeros_like(parts[2]), parts[2])
        taps = dot(jnp.concatenate(parts, axis=1), pc[layer])
        at = lax.broadcasted_iota(jnp.int32, (cols, LANES), 0)
        total = taps[:, LANES : 2 * LANES]
        total += jnp.where(at == first_col, 0.0, pltpu.roll(taps[:, 0:LANES], 1, 0))
        total += jnp.where(at == last_col, 0.0, pltpu.roll(taps[:, 2 * LANES :], cols - 1, 0))
        fed = stream[r // HALF, :, r % HALF].reshape(cols, LANES)
        return fed + (total + small[4 + layer : 5 + layer, :])

    def put0(n, mixed):
        mix0[0, n] = mixed[0:32]
        mix0[1, n] = mixed[32:64]

    def send_odd(g):
        at = pl.ds(g * GROUP, GROUP)
        for half in range(2):
            x = stream[half, at].reshape(GROUP * 32, LANES)
            normed = layer_norm(x, small[2:3, :], channels).astype(BF16).reshape(GROUP, 32, LANES)
            if half == 0:
                bsend[at] = normed
            else:
                kv1[at, pl.ds(0, 32)] = normed
        for copy in odd_copies(g):
            copy.start()

    for g in range(groups + 1):
        if g < groups:
            pair_copy(g).wait_recv()
            attend(0, kv0, g, put0)
            for half in range(2):
                feed(0, mix0, half, g)
                halo_copy(0, half, g).start()
        if g >= 1:
            for side in range(2):
                halo_copy(0, side, g - 1).wait_recv()
            multiply0(g - 1)
        if g >= 2:
            add0(g - 2)
            send_odd(g - 2)
    add0(groups - 1)
    send_odd(groups - 1)
    pad_weights(1)

    def put1(n, mixed):
        mix1[1, n] = mixed[0:32]
        ret[n] = mixed[32:64]

    for g in range(groups):
        for copy in odd_copies(g):
            copy.wait_recv()
        attend(1, kv1, g, put1)
        ret_copy(g).start()
        feed(1, mix1, 1, g)
        if g >= 1:
            ret_copy(g - 1).wait_recv()
            feed(1, mix1, 0, g - 1)
    halo_copy(1, 1).start()

    def finish1(r):
        row = convolve(1, r, cols - HALF, cols - HALF - 1)
        row = pltpu.roll(row.T, HALF, 1)
        xs[pl.ds(r, channels, stride=rows), :] = row[0:channels]

    for r in range(HALF + 1, rows - 1):
        finish1(r)
    ret_copy(groups - 1).wait_recv()
    feed(1, mix1, 0, groups - 1)
    halo_copy(1, 0).start()
    for r in range(1, HALF + 1):
        finish1(r)
    for side in range(2):
        halo_copy(1, side).wait_recv()
    finish1(0)
    finish1(rows - 1)
    out[0] = xs[...].reshape(channels, rows, cols).astype(BF16)

    for g in range(groups):
        pair_copy(g).wait_send()
        for copy in odd_copies(g):
            copy.wait_send()
        ret_copy(g).wait_send()
        for side in range(2):
            halo_copy(0, side, g).wait_send()
    for side in range(2):
        halo_copy(1, side).wait_send()


def on_device(*args):
    frames = args[0]
    _, channels, rows, cols = frames.shape
    windows = cols // WIN
    groups = windows // GROUP
    dma = pltpu.SemaphoreType.DMA
    vmem = pl.BlockSpec(memory_space=pltpu.VMEM)
    return pl.pallas_call(
        kernel,
        out_shape=jax.ShapeDtypeStruct(frames.shape, BF16),
        in_specs=[pl.BlockSpec(memory_space=pltpu.HBM)] * len(args),
        out_specs=vmem,
        scratch_shapes=[pltpu.VMEM(arg.shape, arg.dtype) for arg in args]
        + [
            dma((len(args),)),
            pltpu.VMEM((channels * rows, cols), F32),
            pltpu.VMEM((2, windows, HALF, WIN, LANES), F32),
            pltpu.VMEM((rows, cols + 8, LANES), F32),
            pltpu.VMEM((rows, cols + 8, 384), F32),
            pltpu.VMEM((windows, 128, LANES), BF16),
            pltpu.VMEM((windows, 128, LANES), BF16),
            pltpu.VMEM((windows, 32, LANES), BF16),
            pltpu.VMEM((windows, 32, LANES), BF16),
            pltpu.VMEM((2, windows, 32, LANES), BF16),
            pltpu.VMEM((2, windows, 32, LANES), BF16),
            pltpu.VMEM((rows + 2, cols, LANES), BF16),
            pltpu.VMEM((rows + 2, cols, LANES), BF16),
            pltpu.VMEM((LAYERS, LANES, 384), BF16),
            pltpu.VMEM((LAYERS, LANES, LANES), BF16),
            pltpu.VMEM((LAYERS, LANES, 512), BF16),
            pltpu.VMEM((LAYERS, 256, LANES), BF16),
            pltpu.VMEM((LAYERS, 384, 384), BF16),
            pltpu.VMEM((256, 384), F32),
            pltpu.VMEM((8, LANES), F32),
            dma((groups,)), dma((groups,)),
            dma((3, groups)), dma((3, groups)),
            dma((groups,)), dma((groups,)),
            dma((groups + 1, 2)), dma((groups + 1, 2)),
        ],
        compiler_params=pltpu.CompilerParams(
            collective_id=0, has_side_effects=True, vmem_limit_bytes=63 * 2**20
        ),
    )(*args)


def solution(mesh):
    in_specs = (P(("clips", "tm"), None, "tile", None), P(), P(), P(), P(), P(), P(), P(), P())
    out_specs = P(("clips", "tm"), None, "tile", None)
    return jax.shard_map(
        on_device, mesh=mesh, in_specs=in_specs, out_specs=out_specs, check_vma=False
    )
```

```python
import functools

import jax
import jax.numpy as jnp
from jax import lax
from jax.experimental import pallas as pl
from jax.experimental.pallas import tpu as pltpu
from jax.sharding import PartitionSpec as P

HEADS = 6
HD = 20
LAYERS = 2
LANES = 128
WIN = 8
HALF = WIN // 2
GROUP = 4
F32 = jnp.float32
BF16 = jnp.bfloat16
MESH = pl.DeviceIdType.MESH


def dot(a, b):
    return lax.dot_general(a, b, (((1,), (0,)), ((), ())), preferred_element_type=F32)


def dot_nt(a, b):
    return lax.dot_general(a, b, (((1,), (1,)), ((), ())), preferred_element_type=F32)


def lanes_of(shape):
    return lax.broadcasted_iota(jnp.int32, shape, len(shape) - 1)


def layer_norm(x, gain, channels):
    mean = jnp.sum(x, axis=-1, keepdims=True) * (1.0 / channels)
    center = jnp.where(lanes_of(x.shape) < channels, x - mean, 0.0)
    spread = jnp.sum(center * center, axis=-1, keepdims=True) * (1.0 / channels)
    return center * lax.rsqrt(spread + 1e-05) * gain


def kernel(
    frames_h, ln_gain_h, qkv_h, out_h, gate_h, up_h, down_h, conv_h, conv_b_h, out,
    frames, ln_gain, qkv_w, out_w, gate_w, up_w, down_w, conv_w, conv_b, load_sem,
    xs, stream, fedn, taps, kv0, kv1, bsend, ret, mix0, mix1, yp0, yp1,
    pq, po, pgu, pd, pc, tmp, small,
    send0, recv0, send1, recv1, send_ret, recv_ret, send_halo, recv_halo,
):
    channels, rows, cols = frames.shape[1:]
    hidden = gate_w.shape[2]
    windows = cols // WIN
    groups = windows // GROUP
    span = GROUP * WIN
    tiles, count = lax.axis_size("tile"), lax.axis_size("tm")
    t, f = lax.axis_index("tile"), lax.axis_index("tm")
    odd = lax.rem(f, 2)
    even_pair = f + 1 - 2 * odd
    odd_pair = lax.rem(f + 2 * odd - 1 + count, count)
    above, below = lax.rem(t + tiles - 1, tiles), lax.rem(t + 1, tiles)

    pairs = [
        (frames_h, frames), (ln_gain_h, ln_gain), (conv_b_h, conv_b), (qkv_h, qkv_w), (out_h, out_w),
        (gate_h, gate_w), (up_h, up_w), (down_h, down_w), (conv_h, conv_w),
    ]
    loads = [pltpu.make_async_copy(a, b, load_sem.at[i]) for i, (a, b) in enumerate(pairs)]
    for load in loads:
        load.start()
    barrier = pltpu.get_barrier_semaphore()
    peers = [
        {"tm": even_pair}, {"tm": odd_pair}, {"tile": above}, {"tile": below},
        {"tile": above, "tm": odd_pair}, {"tile": below, "tm": odd_pair},
    ]
    for peer in peers:
        pl.semaphore_signal(barrier, inc=1, device_id=peer, device_id_type=MESH)

    def remote(src, dst, send, recv, peer):
        return pltpu.make_async_remote_copy(
            src_ref=src, dst_ref=dst, send_sem=send, recv_sem=recv,
            device_id=peer, device_id_type=MESH,
        )

    def pair_copy(g):
        at = pl.ds(g * GROUP, GROUP)
        return remote(
            kv0.at[at, pl.ds(0, 64)], kv0.at[at, pl.ds(64, 64)],
            send0.at[g], recv0.at[g], {"tm": even_pair},
        )

    def odd_copies(g):
        at = pl.ds(g * GROUP, GROUP)
        return [
            remote(kv1.at[at, pl.ds(0, 32)], kv1.at[at, pl.ds(64, 32)],
                   send1.at[0, g], recv1.at[0, g], {"tm": odd_pair}),
            remote(bsend.at[at], kv1.at[at, pl.ds(96, 32)],
                   send1.at[1, g], recv1.at[1, g], {"tile": above, "tm": odd_pair}),
            remote(bsend.at[at], kv1.at[at, pl.ds(32, 32)],
                   send1.at[2, g], recv1.at[2, g], {"tile": above}),
        ]

    def ret_copy(g):
        at = pl.ds(g * GROUP, GROUP)
        return remote(ret.at[at], mix1.at[0, at], send_ret.at[g], recv_ret.at[g], {"tile": below})

    def halo_copy(layer, side, g=0):
        yp = (yp0, yp1)[layer]
        at = pl.ds(g * span, span) if layer == 0 else pl.ds(0, cols)
        slot = g if layer == 0 else groups
        if side == 0:
            src, dst, peer = yp.at[1, at], yp.at[rows + 1, at], {"tile": above}
        else:
            src, dst, peer = yp.at[rows, at], yp.at[0, at], {"tile": below}
        return remote(src, dst, send_halo.at[slot, side], recv_halo.at[slot, side], peer)

    for load in loads[0:3]:
        load.wait()
    small[...] = jnp.zeros_like(small)
    for layer in range(LAYERS):
        small[2 * layer : 2 * layer + 2, 0:channels] = ln_gain[layer]
    small[4 : 4 + LAYERS, 0:channels] = conv_b[...]

    xs[...] = frames[0].astype(F32).reshape(channels * rows, cols)
    for r in range(rows):
        row = xs[pl.ds(r, channels, stride=rows), :]
        row = jnp.concatenate([row, jnp.zeros((LANES - channels, cols), F32)], axis=0)
        stream[r // HALF, :, r % HALF] = row.T.reshape(windows, WIN, LANES)

    for g in range(groups):
        at = pl.ds(g * GROUP, GROUP)
        for half in range(2):
            x = stream[half, at].reshape(GROUP * 32, LANES)
            normed = layer_norm(x, small[0:1, :], channels)
            kv0[at, pl.ds(32 * half, 32)] = normed.astype(BF16).reshape(GROUP, 32, LANES)
        if g == 0:
            pl.semaphore_wait(barrier, len(peers))
        pair_copy(g).start()

    for load in loads[3:]:
        load.wait()
    tmp[...] = jnp.zeros_like(tmp)

    def pad_weights(layer):
        tmp[0:channels, 0 : 3 * channels] = qkv_w[layer].astype(F32)
        whole = tmp[0:LANES, 0:384]
        for j in range(3):
            part = whole if j == 0 else pltpu.roll(whole, 384 - channels * j, 1)
            part = part[:, 0:LANES]
            part = jnp.where(lanes_of(part.shape) < channels, part, 0.0)
            part = part if j == 1 else part.T
            pq[layer, :, LANES * j : LANES * (j + 1)] = part.astype(BF16)
        tmp[0:LANES, 0:384] = jnp.zeros((LANES, 384), F32)
        for j, weight in enumerate((gate_w, up_w)):
            tmp[0:channels, 0:hidden] = weight[layer].astype(F32)
            pgu[layer, :, 256 * j : 256 * (j + 1)] = tmp[0:LANES, 0:256].astype(BF16)
        tmp[0:LANES, 0:256] = jnp.zeros((LANES, 256), F32)
        tmp[0:channels, 0:channels] = out_w[layer].astype(F32)
        po[layer] = tmp[0:LANES, 0:LANES].astype(BF16)
        for a in range(3):
            for b in range(3):
                tmp[0:channels, 0:channels] = conv_w[layer, 3 * a + b].astype(F32)
                pc[layer, LANES * a : LANES * (a + 1), LANES * b : LANES * (b + 1)] = tmp[
                    0:LANES, 0:LANES
                ].astype(BF16)
        tmp[0:hidden, 0:channels] = down_w[layer].astype(F32)
        pd[layer] = tmp[0:256, 0:LANES].astype(BF16)
        tmp[0:256, 0:LANES] = jnp.zeros((256, LANES), F32)

    pad_weights(0)

    scale = HD ** (-0.5) * 1.4426950408889634

    def attend(layer, kv, g, put):
        all_in = kv[pl.ds(g * GROUP, GROUP)].reshape(GROUP * 128, LANES)
        keys = dot(all_in, pq[layer, :, LANES : 2 * LANES]).astype(BF16)
        values = dot_nt(pq[layer, :, 2 * LANES : 3 * LANES], all_in)
        ones = jnp.ones((LANES - channels, GROUP * 128), F32)
        values = jnp.concatenate([values[0:channels], ones], axis=0).astype(BF16)
        twice = [all_in[128 * i : 128 * i + 64] for i in range(GROUP) for _ in range(2)]
        queries = dot_nt(pq[layer, :, 0:LANES], jnp.concatenate(twice, axis=0))
        two = 2 * HD
        keep = (lanes_of((two, LANES)) < 64) == (
            lax.broadcasted_iota(jnp.int32, (two, LANES), 0) < HD
        )
        lane = lanes_of((64, LANES))
        first = lane < HD
        for h in range(2, HEADS, 2):
            first |= (lane >= HD * h) & (lane < HD * (h + 1))
        for i in range(GROUP):
            at = slice(128 * i, 128 * (i + 1))
            blocks = []
            for j in range(HEADS // 2):
                block = jnp.where(keep, queries[two * j : two * (j + 1), at], 0.0)
                below_rows = LANES - two * (j + 1)
                pieces = [jnp.zeros((two * j, LANES), F32)] if j else []
                pieces += [block, jnp.zeros((below_rows, LANES), F32)]
                blocks.append(jnp.concatenate(pieces, axis=0))
            spread = jnp.concatenate(blocks, axis=1).astype(BF16)
            scores = dot(keys[at], spread)
            top = jnp.max(scores, axis=0, keepdims=True)
            weights = jnp.exp2((scores - top) * scale).astype(BF16)
            both = dot(values[:, at], weights)
            inverse = 1.0 / both[channels:LANES]
            pieces = []
            for j in range(HEADS // 2):
                cut = slice(LANES * j, LANES * (j + 1))
                for e in range(two * j, two * (j + 1), 8):
                    pieces.append(both[e : e + 8, cut] * inverse[:, cut])
            pieces.append(jnp.zeros((LANES - channels, LANES), F32))
            turned = jnp.concatenate(pieces, axis=0).T
            mixed = jnp.where(first, turned[0:64], turned[64:128]).astype(BF16)
            put(g * GROUP + i, mixed)

    def feed(layer, mix, half, g):
        at = pl.ds(g * GROUP, GROUP)
        x = stream[half, at].reshape(GROUP * 32, LANES)
        x = x + dot(mix[half, at].reshape(GROUP * 32, LANES), po[layer])
        normed = layer_norm(x, small[2 * layer + 1 : 2 * layer + 2, :], channels).astype(BF16)
        gate = dot(normed, pgu[layer, :, 0:256])
        up = dot(normed, pgu[layer, :, 256:512])
        act = 0.5 * gate * (1.0 + lax.erf(gate * 0.7071067811865476)) * up
        x = x + dot(act.astype(BF16), pd[layer])
        stream[half, at] = x.reshape(GROUP, HALF, WIN, LANES)
        for i in range(HALF):
            row = stream[half, at, i].reshape(span, LANES)
            (yp0, yp1)[layer][1 + HALF * half + i, pl.ds(g * span, span)] = row.astype(BF16)
            if layer == 0:
                fedn[HALF * half + i, g * span : (g + 1) * span] = row

    def multiply0(g):
        at = pl.ds(g * span, span)
        lines = [yp0[r, at] for r in range(rows + 2)]
        lines[0] = jnp.where(t == 0, jnp.zeros_like(lines[0]), lines[0])
        lines[-1] = jnp.where(t == tiles - 1, jnp.zeros_like(lines[-1]), lines[-1])
        lhs = [jnp.concatenate(lines[r : r + 3], axis=1) for r in range(rows)]
        result = dot(jnp.concatenate(lhs, axis=0), pc[0])
        for r in range(rows):
            taps[r, g * span : (g + 1) * span] = result[span * r : span * (r + 1)]
            if g == 0:
                taps[r, cols : cols + 8] = result[span * r : span * r + 8]
                fedn[r, cols : cols + 8] = fedn[r, 0:8]

    def add0(g):
        start = g * span + HALF
        at = g * span + lax.broadcasted_iota(jnp.int32, (span, LANES), 0)
        for r in range(rows):
            left = taps[r, start - 1 : start - 1 + span, 0:LANES]
            mid = taps[r, start : start + span, LANES : 2 * LANES]
            right = taps[r, start + 1 : start + 1 + span, 2 * LANES : 3 * LANES]
            left = jnp.where(at == cols - HALF, 0.0, left)
            right = jnp.where(at == cols - HALF - 1, 0.0, right)
            row = fedn[r, start : start + span] + (left + mid + right + small[4:5, :])
            stream[r // HALF, pl.ds(g * GROUP, GROUP), r % HALF] = row.reshape(GROUP, WIN, LANES)

    def convolve(layer, r, first_col, last_col):
        yp = (yp0, yp1)[layer]
        parts = [yp[r], yp[r + 1], yp[r + 2]]
        if r == 0:
            parts[0] = jnp.where(t == 0, jnp.zeros_like(parts[0]), parts[0])
        if r == rows - 1:
            parts[2] = jnp.where(t == tiles - 1, jnp.zeros_like(parts[2]), parts[2])
        taps = dot(jnp.concatenate(parts, axis=1), pc[layer])
        at = lax.broadcasted_iota(jnp.int32, (cols, LANES), 0)
        total = taps[:, LANES : 2 * LANES]
        total += jnp.where(at == first_col, 0.0, pltpu.roll(taps[:, 0:LANES], 1, 0))
        total += jnp.where(at == last_col, 0.0, pltpu.roll(taps[:, 2 * LANES :], cols - 1, 0))
        fed = stream[r // HALF, :, r % HALF].reshape(cols, LANES)
        return fed + (total + small[4 + layer : 5 + layer, :])

    def put0(n, mixed):
        mix0[0, n] = mixed[0:32]
        mix0[1, n] = mixed[32:64]

    def send_odd(g):
        at = pl.ds(g * GROUP, GROUP)
        for half in range(2):
            x = stream[half, at].reshape(GROUP * 32, LANES)
            normed = layer_norm(x, small[2:3, :], channels).astype(BF16).reshape(GROUP, 32, LANES)
            if half == 0:
                bsend[at] = normed
            else:
                kv1[at, pl.ds(0, 32)] = normed
        for copy in odd_copies(g):
            copy.start()

    for g in range(groups + 1):
        if g < groups:
            pair_copy(g).wait_recv()
            attend(0, kv0, g, put0)
            for half in range(2):
                feed(0, mix0, half, g)
                halo_copy(0, half, g).start()
        if g >= 1:
            for side in range(2):
                halo_copy(0, side, g - 1).wait_recv()
            multiply0(g - 1)
        if g >= 2:
            add0(g - 2)
            send_odd(g - 2)
    add0(groups - 1)
    send_odd(groups - 1)
    pad_weights(1)

    def put1(n, mixed):
        mix1[1, n] = mixed[0:32]
        ret[n] = mixed[32:64]

    for g in range(groups):
        for copy in odd_copies(g):
            copy.wait_recv()
        attend(1, kv1, g, put1)
        ret_copy(g).start()
        feed(1, mix1, 1, g)
        if g >= 1:
            ret_copy(g - 1).wait_recv()
            feed(1, mix1, 0, g - 1)
    halo_copy(1, 1).start()

    def finish1(r):
        row = convolve(1, r, cols - HALF, cols - HALF - 1)
        row = pltpu.roll(row.T, HALF, 1)
        xs[pl.ds(r, channels, stride=rows), :] = row[0:channels]

    for r in range(HALF + 1, rows - 1):
        finish1(r)
    ret_copy(groups - 1).wait_recv()
    feed(1, mix1, 0, groups - 1)
    halo_copy(1, 0).start()
    for r in range(1, HALF + 1):
        finish1(r)
    for side in range(2):
        halo_copy(1, side).wait_recv()
    finish1(0)
    finish1(rows - 1)
    out[0] = xs[...].reshape(channels, rows, cols).astype(BF16)

    for g in range(groups):
        pair_copy(g).wait_send()
        for copy in odd_copies(g):
            copy.wait_send()
        ret_copy(g).wait_send()
        for side in range(2):
            halo_copy(0, side, g).wait_send()
    for side in range(2):
        halo_copy(1, side).wait_send()


def on_device(*args):
    frames = args[0]
    _, channels, rows, cols = frames.shape
    windows = cols // WIN
    groups = windows // GROUP
    dma = pltpu.SemaphoreType.DMA
    vmem = pl.BlockSpec(memory_space=pltpu.VMEM)
    return pl.pallas_call(
        kernel,
        out_shape=jax.ShapeDtypeStruct(frames.shape, BF16),
        in_specs=[pl.BlockSpec(memory_space=pltpu.HBM)] * len(args),
        out_specs=vmem,
        scratch_shapes=[pltpu.VMEM(arg.shape, arg.dtype) for arg in args]
        + [
            dma((len(args),)),
            pltpu.VMEM((channels * rows, cols), F32),
            pltpu.VMEM((2, windows, HALF, WIN, LANES), F32),
            pltpu.VMEM((rows, cols + 8, LANES), F32),
            pltpu.VMEM((rows, cols + 8, 384), F32),
            pltpu.VMEM((windows, 128, LANES), BF16),
            pltpu.VMEM((windows, 128, LANES), BF16),
            pltpu.VMEM((windows, 32, LANES), BF16),
            pltpu.VMEM((windows, 32, LANES), BF16),
            pltpu.VMEM((2, windows, 32, LANES), BF16),
            pltpu.VMEM((2, windows, 32, LANES), BF16),
            pltpu.VMEM((rows + 2, cols, LANES), BF16),
            pltpu.VMEM((rows + 2, cols, LANES), BF16),
            pltpu.VMEM((LAYERS, LANES, 384), BF16),
            pltpu.VMEM((LAYERS, LANES, LANES), BF16),
            pltpu.VMEM((LAYERS, LANES, 512), BF16),
            pltpu.VMEM((LAYERS, 256, LANES), BF16),
            pltpu.VMEM((LAYERS, 384, 384), BF16),
            pltpu.VMEM((256, 384), F32),
            pltpu.VMEM((8, LANES), F32),
            dma((groups,)), dma((groups,)),
            dma((3, groups)), dma((3, groups)),
            dma((groups,)), dma((groups,)),
            dma((groups + 1, 2)), dma((groups + 1, 2)),
        ],
        compiler_params=pltpu.CompilerParams(
            collective_id=0, has_side_effects=True, vmem_limit_bytes=63 * 2**20
        ),
    )(*args)


def solution(mesh):
    in_specs = (P(("clips", "tm"), None, "tile", None), P(), P(), P(), P(), P(), P(), P(), P())
    out_specs = P(("clips", "tm"), None, "tile", None)
    return jax.shard_map(
        on_device, mesh=mesh, in_specs=in_specs, out_specs=out_specs, check_vma=False
    )
```

```python
import functools

import jax
import jax.numpy as jnp
from jax import lax
from jax.experimental import pallas as pl
from jax.experimental.pallas import tpu as pltpu
from jax.sharding import PartitionSpec as P

HEADS = 6
HD = 20
LAYERS = 2
LANES = 128
WIN = 8
HALF = WIN // 2
GROUP = 4
F32 = jnp.float32
BF16 = jnp.bfloat16
MESH = pl.DeviceIdType.MESH


def dot(a, b):
    return lax.dot_general(a, b, (((1,), (0,)), ((), ())), preferred_element_type=F32)


def dot_nt(a, b):
    return lax.dot_general(a, b, (((1,), (1,)), ((), ())), preferred_element_type=F32)


def lanes_of(shape):
    return lax.broadcasted_iota(jnp.int32, shape, len(shape) - 1)


def layer_norm(x, gain, channels):
    mean = jnp.sum(x, axis=-1, keepdims=True) * (1.0 / channels)
    center = jnp.where(lanes_of(x.shape) < channels, x - mean, 0.0)
    spread = jnp.sum(center * center, axis=-1, keepdims=True) * (1.0 / channels)
    return center * lax.rsqrt(spread + 1e-05) * gain


def kernel(
    frames_h, ln_gain_h, qkv_h, out_h, gate_h, up_h, down_h, conv_h, conv_b_h, out,
    frames, ln_gain, qkv_w, out_w, gate_w, up_w, down_w, conv_w, conv_b, load_sem,
    xs, stream, fedn, taps, final, kv0, kv1, bsend, ret, mix0, mix1, yp0, yp1,
    pq, po, pgu, pd, pc, tmp, small,
    send0, recv0, send1, recv1, send_ret, recv_ret, send_halo, recv_halo,
):
    channels, rows, cols = frames.shape[1:]
    hidden = gate_w.shape[2]
    windows = cols // WIN
    groups = windows // GROUP
    span = GROUP * WIN
    tiles, count = lax.axis_size("tile"), lax.axis_size("tm")
    t, f = lax.axis_index("tile"), lax.axis_index("tm")
    odd = lax.rem(f, 2)
    even_pair = f + 1 - 2 * odd
    odd_pair = lax.rem(f + 2 * odd - 1 + count, count)
    above, below = lax.rem(t + tiles - 1, tiles), lax.rem(t + 1, tiles)

    pairs = [
        (frames_h, frames), (ln_gain_h, ln_gain), (conv_b_h, conv_b), (qkv_h, qkv_w), (out_h, out_w),
        (gate_h, gate_w), (up_h, up_w), (down_h, down_w), (conv_h, conv_w),
    ]
    loads = [pltpu.make_async_copy(a, b, load_sem.at[i]) for i, (a, b) in enumerate(pairs)]
    for load in loads:
        load.start()
    barrier = pltpu.get_barrier_semaphore()
    peers = [
        {"tm": even_pair}, {"tm": odd_pair}, {"tile": above}, {"tile": below},
        {"tile": above, "tm": odd_pair}, {"tile": below, "tm": odd_pair},
    ]
    for peer in peers:
        pl.semaphore_signal(barrier, inc=1, device_id=peer, device_id_type=MESH)

    def remote(src, dst, send, recv, peer):
        return pltpu.make_async_remote_copy(
            src_ref=src, dst_ref=dst, send_sem=send, recv_sem=recv,
            device_id=peer, device_id_type=MESH,
        )

    def pair_copy(g):
        at = pl.ds(g * GROUP, GROUP)
        return remote(
            kv0.at[at, pl.ds(0, 64)], kv0.at[at, pl.ds(64, 64)],
            send0.at[g], recv0.at[g], {"tm": even_pair},
        )

    def odd_copies(g):
        at = pl.ds(g * GROUP, GROUP)
        return [
            remote(kv1.at[at, pl.ds(0, 32)], kv1.at[at, pl.ds(64, 32)],
                   send1.at[0, g], recv1.at[0, g], {"tm": odd_pair}),
            remote(bsend.at[at], kv1.at[at, pl.ds(96, 32)],
                   send1.at[1, g], recv1.at[1, g], {"tile": above, "tm": odd_pair}),
            remote(bsend.at[at], kv1.at[at, pl.ds(32, 32)],
                   send1.at[2, g], recv1.at[2, g], {"tile": above}),
        ]

    def ret_copy(g):
        at = pl.ds(g * GROUP, GROUP)
        return remote(ret.at[at], mix1.at[0, at], send_ret.at[g], recv_ret.at[g], {"tile": below})

    def halo_copy(layer, side, g):
        yp = (yp0, yp1)[layer]
        at = pl.ds(g * span, span)
        slot = layer * groups + g
        if side == 0:
            src, dst, peer = yp.at[1, at], yp.at[rows + 1, at], {"tile": above}
        else:
            src, dst, peer = yp.at[rows, at], yp.at[0, at], {"tile": below}
        return remote(src, dst, send_halo.at[slot, side], recv_halo.at[slot, side], peer)

    for load in loads[0:3]:
        load.wait()
    small[...] = jnp.zeros_like(small)
    for layer in range(LAYERS):
        small[2 * layer : 2 * layer + 2, 0:channels] = ln_gain[layer]
    small[4 : 4 + LAYERS, 0:channels] = conv_b[...]

    xs[...] = frames[0].astype(F32).reshape(channels * rows, cols)
    for r in range(rows):
        row = xs[pl.ds(r, channels, stride=rows), :]
        row = jnp.concatenate([row, jnp.zeros((LANES - channels, cols), F32)], axis=0)
        stream[r // HALF, :, r % HALF] = row.T.reshape(windows, WIN, LANES)

    for g in range(groups):
        at = pl.ds(g * GROUP, GROUP)
        for half in range(2):
            x = stream[half, at].reshape(GROUP * 32, LANES)
            normed = layer_norm(x, small[0:1, :], channels)
            kv0[at, pl.ds(32 * half, 32)] = normed.astype(BF16).reshape(GROUP, 32, LANES)
        if g == 0:
            pl.semaphore_wait(barrier, len(peers))
        pair_copy(g).start()

    for load in loads[3:]:
        load.wait()
    tmp[...] = jnp.zeros_like(tmp)

    def pad_weights(layer):
        tmp[0:channels, 0 : 3 * channels] = qkv_w[layer].astype(F32)
        whole = tmp[0:LANES, 0:384]
        for j in range(3):
            part = whole if j == 0 else pltpu.roll(whole, 384 - channels * j, 1)
            part = part[:, 0:LANES]
            part = jnp.where(lanes_of(part.shape) < channels, part, 0.0)
            pq[layer, :, LANES * j : LANES * (j + 1)] = part.astype(BF16)
        tmp[0:LANES, 0:384] = jnp.zeros((LANES, 384), F32)
        for j, weight in enumerate((gate_w, up_w)):
            tmp[0:channels, 0:hidden] = weight[layer].astype(F32)
            pgu[layer, :, 256 * j : 256 * (j + 1)] = tmp[0:LANES, 0:256].astype(BF16)
        tmp[0:LANES, 0:256] = jnp.zeros((LANES, 256), F32)
        tmp[0:channels, 0:channels] = out_w[layer].astype(F32)
        po[layer] = tmp[0:LANES, 0:LANES].astype(BF16)
        for a in range(3):
            for b in range(3):
                tmp[0:channels, 0:channels] = conv_w[layer, 3 * a + b].astype(F32)
                pc[layer, LANES * a : LANES * (a + 1), LANES * b : LANES * (b + 1)] = tmp[
                    0:LANES, 0:LANES
                ].astype(BF16)
        tmp[0:hidden, 0:channels] = down_w[layer].astype(F32)
        pd[layer] = tmp[0:256, 0:LANES].astype(BF16)
        tmp[0:256, 0:LANES] = jnp.zeros((256, LANES), F32)

    pad_weights(0)

    scale = HD ** (-0.5) * 1.4426950408889634

    def attend(layer, kv, g, put):
        at = pl.ds(g * GROUP, GROUP)
        all_in = kv[at].reshape(GROUP * 128, LANES)
        q_in = kv[at, pl.ds(0, 64)].reshape(GROUP * 64, LANES)
        packed = dot(all_in, pq[layer, :, LANES:384]).astype(BF16)
        queries = dot(q_in, pq[layer, :, 0:LANES]).astype(BF16).astype(F32)
        lane = lanes_of((64, LANES))
        head = [(lane >= HD * h) & (lane < HD * (h + 1)) for h in range(HEADS)]
        ones = jnp.ones((128, LANES), BF16)
        for i in range(GROUP):
            q = queries[64 * i : 64 * (i + 1)]
            q = jnp.concatenate([jnp.where(head[h], q, 0.0).astype(BF16) for h in range(HEADS)], axis=0)
            k = packed[128 * i : 128 * (i + 1), 0:LANES]
            v = jnp.concatenate([packed[128 * i : 128 * (i + 1), LANES:256], ones], axis=1)
            scores = dot_nt(q, k)
            top = jnp.max(scores, axis=-1, keepdims=True)
            weights = jnp.exp2((scores - top) * scale).astype(BF16)
            both = dot(weights, v)
            mixed, total = both[0:64, 0:LANES], both[0:64, LANES:256]
            for h in range(1, HEADS):
                mixed = jnp.where(head[h], both[64 * h : 64 * (h + 1), 0:LANES], mixed)
                total = jnp.where(head[h], both[64 * h : 64 * (h + 1), LANES:256], total)
            mixed = (mixed / total).astype(BF16)
            put(g * GROUP + i, mixed)

    def feed(layer, mix, half, g):
        at = pl.ds(g * GROUP, GROUP)
        x = stream[half, at].reshape(GROUP * 32, LANES)
        x = x + dot(mix[half, at].reshape(GROUP * 32, LANES), po[layer])
        normed = layer_norm(x, small[2 * layer + 1 : 2 * layer + 2, :], channels).astype(BF16)
        gate = dot(normed, pgu[layer, :, 0:256])
        up = dot(normed, pgu[layer, :, 256:512])
        act = 0.5 * gate * (1.0 + lax.erf(gate * 0.7071067811865476)) * up
        x = x + dot(act.astype(BF16), pd[layer])
        stream[half, at] = x.reshape(GROUP, HALF, WIN, LANES)
        for i in range(HALF):
            row = stream[half, at, i].reshape(span, LANES)
            (yp0, yp1)[layer][1 + HALF * half + i, pl.ds(g * span, span)] = row.astype(BF16)
            off = 8 * layer + g * span
            fedn[HALF * half + i, off : off + span] = row

    def multiply(layer, g):
        at = pl.ds(g * span, span)
        lines = [(yp0, yp1)[layer][r, at] for r in range(rows + 2)]
        lines[0] = jnp.where(t == 0, jnp.zeros_like(lines[0]), lines[0])
        lines[-1] = jnp.where(t == tiles - 1, jnp.zeros_like(lines[-1]), lines[-1])
        lhs = [jnp.concatenate(lines[r : r + 3], axis=1) for r in range(rows)]
        result = dot(jnp.concatenate(lhs, axis=0), pc[layer])
        off = 8 * layer + g * span
        for r in range(rows):
            taps[r, off : off + span] = result[span * r : span * (r + 1)]
            if layer == 1 and g == groups - 1:
                taps[r, 0:8] = result[span * (r + 1) - 8 : span * (r + 1)]
                fedn[r, 0:8] = fedn[r, cols : cols + 8]
            if layer == 0 and g == 0:
                taps[r, cols : cols + 8] = result[span * r : span * r + 8]
                fedn[r, cols : cols + 8] = fedn[r, 0:8]

    def add0(g):
        start = g * span + HALF
        at = g * span + lax.broadcasted_iota(jnp.int32, (span, LANES), 0)
        for r in range(rows):
            left = taps[r, start - 1 : start - 1 + span, 0:LANES]
            mid = taps[r, start : start + span, LANES : 2 * LANES]
            right = taps[r, start + 1 : start + 1 + span, 2 * LANES : 3 * LANES]
            left = jnp.where(at == cols - HALF, 0.0, left)
            right = jnp.where(at == cols - HALF - 1, 0.0, right)
            row = fedn[r, start : start + span] + (left + mid + right + small[4:5, :])
            stream[r // HALF, pl.ds(g * GROUP, GROUP), r % HALF] = row.reshape(GROUP, WIN, LANES)

    def add1(g):
        start = g * span + HALF
        at = g * span + lax.broadcasted_iota(jnp.int32, (span, LANES), 0)
        for r in range(rows):
            left = taps[r, start - 1 : start - 1 + span, 0:LANES]
            mid = taps[r, start : start + span, LANES : 2 * LANES]
            right = taps[r, start + 1 : start + 1 + span, 2 * LANES : 3 * LANES]
            if g == 0:
                left = jnp.where(at == 0, 0.0, left)
            if g == groups - 1:
                right = jnp.where(at == cols - 1, 0.0, right)
            row = fedn[r, start : start + span] + (left + mid + right + small[5:6, :])
            final[r, g * span : (g + 1) * span] = row

    def put0(n, mixed):
        mix0[0, n] = mixed[0:32]
        mix0[1, n] = mixed[32:64]

    def send_odd(g):
        at = pl.ds(g * GROUP, GROUP)
        for half in range(2):
            x = stream[half, at].reshape(GROUP * 32, LANES)
            normed = layer_norm(x, small[2:3, :], channels).astype(BF16).reshape(GROUP, 32, LANES)
            if half == 0:
                bsend[at] = normed
            else:
                kv1[at, pl.ds(0, 32)] = normed
        for copy in odd_copies(g):
            copy.start()

    for g in range(groups + 1):
        if g < groups:
            pair_copy(g).wait_recv()
            attend(0, kv0, g, put0)
        if g >= 1:
            for side in range(2):
                halo_copy(0, side, g - 1).wait_recv()
            multiply(0, g - 1)
        if g >= 2:
            add0(g - 2)
            send_odd(g - 2)
        if g < groups:
            for half in range(2):
                feed(0, mix0, half, g)
                halo_copy(0, half, g).start()
    add0(groups - 1)
    send_odd(groups - 1)
    pad_weights(1)

    def put1(n, mixed):
        mix1[1, n] = mixed[0:32]
        ret[n] = mixed[32:64]

    for g in range(groups + 2):
        if g < groups:
            for copy in odd_copies(g):
                copy.wait_recv()
            attend(1, kv1, g, put1)
            ret_copy(g).start()
            feed(1, mix1, 1, g)
            halo_copy(1, 1, g).start()
        if 1 <= g <= groups:
            ret_copy(g - 1).wait_recv()
            feed(1, mix1, 0, g - 1)
            halo_copy(1, 0, g - 1).start()
        if g >= 2:
            for side in range(2):
                halo_copy(1, side, g - 2).wait_recv()
            multiply(1, g - 2)
            if g >= 3:
                add1(g - 2)
    add1(0)
    for r in range(rows):
        xs[pl.ds(r, channels, stride=rows), :] = final[r].T[0:channels]
    out[0] = xs[...].reshape(channels, rows, cols).astype(BF16)

    for g in range(groups):
        pair_copy(g).wait_send()
        for copy in odd_copies(g):
            copy.wait_send()
        ret_copy(g).wait_send()
        for side in range(2):
            halo_copy(0, side, g).wait_send()
            halo_copy(1, side, g).wait_send()


def on_device(*args):
    frames = args[0]
    _, channels, rows, cols = frames.shape
    windows = cols // WIN
    groups = windows // GROUP
    dma = pltpu.SemaphoreType.DMA
    vmem = pl.BlockSpec(memory_space=pltpu.VMEM)
    return pl.pallas_call(
        kernel,
        out_shape=jax.ShapeDtypeStruct(frames.shape, BF16),
        in_specs=[pl.BlockSpec(memory_space=pltpu.HBM)] * len(args),
        out_specs=vmem,
        scratch_shapes=[pltpu.VMEM(arg.shape, arg.dtype) for arg in args]
        + [
            dma((len(args),)),
            pltpu.VMEM((channels * rows, cols), F32),
            pltpu.VMEM((2, windows, HALF, WIN, LANES), F32),
            pltpu.VMEM((rows, cols + 8, LANES), F32),
            pltpu.VMEM((rows, cols + 8, 384), F32),
            pltpu.VMEM((rows, cols, LANES), F32),
            pltpu.VMEM((windows, 128, LANES), BF16),
            pltpu.VMEM((windows, 128, LANES), BF16),
            pltpu.VMEM((windows, 32, LANES), BF16),
            pltpu.VMEM((windows, 32, LANES), BF16),
            pltpu.VMEM((2, windows, 32, LANES), BF16),
            pltpu.VMEM((2, windows, 32, LANES), BF16),
            pltpu.VMEM((rows + 2, cols, LANES), BF16),
            pltpu.VMEM((rows + 2, cols, LANES), BF16),
            pltpu.VMEM((LAYERS, LANES, 384), BF16),
            pltpu.VMEM((LAYERS, LANES, LANES), BF16),
            pltpu.VMEM((LAYERS, LANES, 512), BF16),
            pltpu.VMEM((LAYERS, 256, LANES), BF16),
            pltpu.VMEM((LAYERS, 384, 384), BF16),
            pltpu.VMEM((256, 384), F32),
            pltpu.VMEM((8, LANES), F32),
            dma((groups,)), dma((groups,)),
            dma((3, groups)), dma((3, groups)),
            dma((groups,)), dma((groups,)),
            dma((LAYERS * groups, 2)), dma((LAYERS * groups, 2)),
        ],
        compiler_params=pltpu.CompilerParams(
            collective_id=0, has_side_effects=True, vmem_limit_bytes=63 * 2**20
        ),
    )(*args)


def solution(mesh):
    in_specs = (P(("clips", "tm"), None, "tile", None), P(), P(), P(), P(), P(), P(), P(), P())
    out_specs = P(("clips", "tm"), None, "tile", None)
    return jax.shard_map(
        on_device, mesh=mesh, in_specs=in_specs, out_specs=out_specs, check_vma=False
    )
```

```python
import functools

import jax
import jax.numpy as jnp
from jax import lax
from jax.experimental import pallas as pl
from jax.experimental.pallas import tpu as pltpu
from jax.sharding import PartitionSpec as P

HEADS = 6
HD = 20
LAYERS = 2
LANES = 128
WIN = 8
HALF = WIN // 2
GROUP = 4
F32 = jnp.float32
BF16 = jnp.bfloat16
MESH = pl.DeviceIdType.MESH


def dot(a, b):
    return lax.dot_general(a, b, (((1,), (0,)), ((), ())), preferred_element_type=F32)


def dot_nt(a, b):
    return lax.dot_general(a, b, (((1,), (1,)), ((), ())), preferred_element_type=F32)


def lanes_of(shape):
    return lax.broadcasted_iota(jnp.int32, shape, len(shape) - 1)


def layer_norm(x, gain, channels):
    mean = jnp.sum(x, axis=-1, keepdims=True) * (1.0 / channels)
    center = jnp.where(lanes_of(x.shape) < channels, x - mean, 0.0)
    spread = jnp.sum(center * center, axis=-1, keepdims=True) * (1.0 / channels)
    return center * lax.rsqrt(spread + 1e-05) * gain


def kernel(
    frames_h, ln_gain_h, qkv_h, out_h, gate_h, up_h, down_h, conv_h, conv_b_h, out,
    frames, ln_gain, qkv_w, out_w, gate_w, up_w, down_w, conv_w, conv_b, load_sem,
    xs, stream, fedn, taps, kv0, kv1, bsend, ret, mix0, mix1, yp0, yp1,
    pq, po, pgu, pd, pc, tmp, small,
    send0, recv0, send1, recv1, send_ret, recv_ret, send_halo, recv_halo,
):
    channels, rows, cols = frames.shape[1:]
    hidden = gate_w.shape[2]
    windows = cols // WIN
    groups = windows // GROUP
    span = GROUP * WIN
    tiles, count = lax.axis_size("tile"), lax.axis_size("tm")
    t, f = lax.axis_index("tile"), lax.axis_index("tm")
    odd = lax.rem(f, 2)
    even_pair = f + 1 - 2 * odd
    odd_pair = lax.rem(f + 2 * odd - 1 + count, count)
    above, below = lax.rem(t + tiles - 1, tiles), lax.rem(t + 1, tiles)

    pairs = [
        (frames_h, frames), (ln_gain_h, ln_gain), (conv_b_h, conv_b), (qkv_h, qkv_w), (out_h, out_w),
        (gate_h, gate_w), (up_h, up_w), (down_h, down_w), (conv_h, conv_w),
    ]
    loads = [pltpu.make_async_copy(a, b, load_sem.at[i]) for i, (a, b) in enumerate(pairs)]
    for load in loads:
        load.start()
    barrier = pltpu.get_barrier_semaphore()
    peers = [
        {"tm": even_pair}, {"tm": odd_pair}, {"tile": above}, {"tile": below},
        {"tile": above, "tm": odd_pair}, {"tile": below, "tm": odd_pair},
    ]
    for peer in peers:
        pl.semaphore_signal(barrier, inc=1, device_id=peer, device_id_type=MESH)

    def remote(src, dst, send, recv, peer):
        return pltpu.make_async_remote_copy(
            src_ref=src, dst_ref=dst, send_sem=send, recv_sem=recv,
            device_id=peer, device_id_type=MESH,
        )

    def pair_copy(g):
        at = pl.ds(g * GROUP, GROUP)
        return remote(
            kv0.at[at, pl.ds(0, 64)], kv0.at[at, pl.ds(64, 64)],
            send0.at[g], recv0.at[g], {"tm": even_pair},
        )

    def odd_copies(g):
        at = pl.ds(g * GROUP, GROUP)
        return [
            remote(kv1.at[at, pl.ds(0, 32)], kv1.at[at, pl.ds(64, 32)],
                   send1.at[0, g], recv1.at[0, g], {"tm": odd_pair}),
            remote(bsend.at[at], kv1.at[at, pl.ds(96, 32)],
                   send1.at[1, g], recv1.at[1, g], {"tile": above, "tm": odd_pair}),
            remote(bsend.at[at], kv1.at[at, pl.ds(32, 32)],
                   send1.at[2, g], recv1.at[2, g], {"tile": above}),
        ]

    def ret_copy(g):
        at = pl.ds(g * GROUP, GROUP)
        return remote(ret.at[at], mix1.at[0, at], send_ret.at[g], recv_ret.at[g], {"tile": below})

    def halo_copy(layer, side, g=0):
        yp = (yp0, yp1)[layer]
        at = pl.ds(g * span, span) if layer == 0 else pl.ds(0, cols)
        slot = g if layer == 0 else groups
        if side == 0:
            src, dst, peer = yp.at[1, at], yp.at[rows + 1, at], {"tile": above}
        else:
            src, dst, peer = yp.at[rows, at], yp.at[0, at], {"tile": below}
        return remote(src, dst, send_halo.at[slot, side], recv_halo.at[slot, side], peer)

    for load in loads[0:3]:
        load.wait()
    small[...] = jnp.zeros_like(small)
    for layer in range(LAYERS):
        small[2 * layer : 2 * layer + 2, 0:channels] = ln_gain[layer]
    small[4 : 4 + LAYERS, 0:channels] = conv_b[...]

    xs[...] = frames[0].astype(F32).reshape(channels * rows, cols)
    for r in range(rows):
        row = xs[pl.ds(r, channels, stride=rows), :]
        row = jnp.concatenate([row, jnp.zeros((LANES - channels, cols), F32)], axis=0)
        stream[r // HALF, :, r % HALF] = row.T.reshape(windows, WIN, LANES)

    for g in range(groups):
        at = pl.ds(g * GROUP, GROUP)
        for half in range(2):
            x = stream[half, at].reshape(GROUP * 32, LANES)
            normed = layer_norm(x, small[0:1, :], channels)
            kv0[at, pl.ds(32 * half, 32)] = normed.astype(BF16).reshape(GROUP, 32, LANES)
        if g == 0:
            pl.semaphore_wait(barrier, len(peers))
        pair_copy(g).start()

    for load in loads[3:]:
        load.wait()
    tmp[...] = jnp.zeros_like(tmp)

    def pad_weights(layer):
        tmp[0:channels, 0 : 3 * channels] = qkv_w[layer].astype(F32)
        whole = tmp[0:LANES, 0:384]
        for j in range(3):
            part = whole if j == 0 else pltpu.roll(whole, 384 - channels * j, 1)
            part = part[:, 0:LANES]
            part = jnp.where(lanes_of(part.shape) < channels, part, 0.0)
            pq[layer, :, LANES * j : LANES * (j + 1)] = part.astype(BF16)
        tmp[0:LANES, 0:384] = jnp.zeros((LANES, 384), F32)
        for j, weight in enumerate((gate_w, up_w)):
            tmp[0:channels, 0:hidden] = weight[layer].astype(F32)
            pgu[layer, :, 256 * j : 256 * (j + 1)] = tmp[0:LANES, 0:256].astype(BF16)
        tmp[0:LANES, 0:256] = jnp.zeros((LANES, 256), F32)
        tmp[0:channels, 0:channels] = out_w[layer].astype(F32)
        po[layer] = tmp[0:LANES, 0:LANES].astype(BF16)
        for a in range(3):
            for b in range(3):
                tmp[0:channels, 0:channels] = conv_w[layer, 3 * a + b].astype(F32)
                pc[layer, LANES * a : LANES * (a + 1), LANES * b : LANES * (b + 1)] = tmp[
                    0:LANES, 0:LANES
                ].astype(BF16)
        tmp[0:hidden, 0:channels] = down_w[layer].astype(F32)
        pd[layer] = tmp[0:256, 0:LANES].astype(BF16)
        tmp[0:256, 0:LANES] = jnp.zeros((256, LANES), F32)

    pad_weights(0)

    scale = HD ** (-0.5) * 1.4426950408889634

    def attend(layer, kv, g, put):
        at = pl.ds(g * GROUP, GROUP)
        all_in = kv[at].reshape(GROUP * 128, LANES)
        q_in = kv[at, pl.ds(0, 64)].reshape(GROUP * 64, LANES)
        packed = dot(all_in, pq[layer, :, LANES:384]).astype(BF16)
        queries = dot(q_in, pq[layer, :, 0:LANES]).astype(BF16).astype(F32)
        lane = lanes_of((64, LANES))
        head = [(lane >= HD * h) & (lane < HD * (h + 1)) for h in range(HEADS)]
        ones = jnp.ones((128, LANES), BF16)
        for i in range(GROUP):
            q = queries[64 * i : 64 * (i + 1)]
            q = jnp.concatenate([jnp.where(head[h], q, 0.0).astype(BF16) for h in range(HEADS)], axis=0)
            k = packed[128 * i : 128 * (i + 1), 0:LANES]
            v = jnp.concatenate([packed[128 * i : 128 * (i + 1), LANES:256], ones], axis=1)
            scores = dot_nt(q, k)
            top = jnp.max(scores, axis=-1, keepdims=True)
            weights = jnp.exp2((scores - top) * scale).astype(BF16)
            both = dot(weights, v)
            mixed, total = both[0:64, 0:LANES], both[0:64, LANES:256]
            for h in range(1, HEADS):
                mixed = jnp.where(head[h], both[64 * h : 64 * (h + 1), 0:LANES], mixed)
                total = jnp.where(head[h], both[64 * h : 64 * (h + 1), LANES:256], total)
            mixed = (mixed / total).astype(BF16)
            put(g * GROUP + i, mixed)

    def feed(layer, mix, half, g):
        at = pl.ds(g * GROUP, GROUP)
        x = stream[half, at].reshape(GROUP * 32, LANES)
        x = x + dot(mix[half, at].reshape(GROUP * 32, LANES), po[layer])
        normed = layer_norm(x, small[2 * layer + 1 : 2 * layer + 2, :], channels).astype(BF16)
        gate = dot(normed, pgu[layer, :, 0:256])
        up = dot(normed, pgu[layer, :, 256:512])
        act = 0.5 * gate * (1.0 + lax.erf(gate * 0.7071067811865476)) * up
        x = x + dot(act.astype(BF16), pd[layer])
        stream[half, at] = x.reshape(GROUP, HALF, WIN, LANES)
        for i in range(HALF):
            row = stream[half, at, i].reshape(span, LANES)
            (yp0, yp1)[layer][1 + HALF * half + i, pl.ds(pl.multiple_of(g * span, span) if layer else g * span, span)] = row.astype(BF16)
            if layer == 0:
                fedn[HALF * half + i, g * span : (g + 1) * span] = row

    def multiply0(g):
        at = pl.ds(g * span, span)
        lines = [yp0[r, at] for r in range(rows + 2)]
        lines[0] = jnp.where(t == 0, jnp.zeros_like(lines[0]), lines[0])
        lines[-1] = jnp.where(t == tiles - 1, jnp.zeros_like(lines[-1]), lines[-1])
        lhs = [jnp.concatenate(lines[r : r + 3], axis=1) for r in range(rows)]
        result = dot(jnp.concatenate(lhs, axis=0), pc[0])
        for r in range(rows):
            taps[r, g * span : (g + 1) * span] = result[span * r : span * (r + 1)]
            if g == 0:
                taps[r, cols : cols + 8] = result[span * r : span * r + 8]
                fedn[r, cols : cols + 8] = fedn[r, 0:8]

    def add0(g):
        start = g * span + HALF
        at = g * span + lax.broadcasted_iota(jnp.int32, (span, LANES), 0)
        for r in range(rows):
            left = taps[r, start - 1 : start - 1 + span, 0:LANES]
            mid = taps[r, start : start + span, LANES : 2 * LANES]
            right = taps[r, start + 1 : start + 1 + span, 2 * LANES : 3 * LANES]
            left = jnp.where(at == cols - HALF, 0.0, left)
            right = jnp.where(at == cols - HALF - 1, 0.0, right)
            row = fedn[r, start : start + span] + (left + mid + right + small[4:5, :])
            stream[r // HALF, pl.ds(g * GROUP, GROUP), r % HALF] = row.reshape(GROUP, WIN, LANES)

    def convolve(layer, r, first_col, last_col):
        yp = (yp0, yp1)[layer]
        parts = [yp[r], yp[r + 1], yp[r + 2]]
        if r == 0:
            parts[0] = jnp.where(t == 0, jnp.zeros_like(parts[0]), parts[0])
        if r == rows - 1:
            parts[2] = jnp.where(t == tiles - 1, jnp.zeros_like(parts[2]), parts[2])
        taps = dot(jnp.concatenate(parts, axis=1), pc[layer])
        at = lax.broadcasted_iota(jnp.int32, (cols, LANES), 0)
        total = taps[:, LANES : 2 * LANES]
        total += jnp.where(at == first_col, 0.0, pltpu.roll(taps[:, 0:LANES], 1, 0))
        total += jnp.where(at == last_col, 0.0, pltpu.roll(taps[:, 2 * LANES :], cols - 1, 0))
        fed = stream[r // HALF, :, r % HALF].reshape(cols, LANES)
        return fed + (total + small[4 + layer : 5 + layer, :])

    def put0(n, mixed):
        mix0[0, n] = mixed[0:32]
        mix0[1, n] = mixed[32:64]

    def send_odd(g):
        at = pl.ds(g * GROUP, GROUP)
        for half in range(2):
            x = stream[half, at].reshape(GROUP * 32, LANES)
            normed = layer_norm(x, small[2:3, :], channels).astype(BF16).reshape(GROUP, 32, LANES)
            if half == 0:
                bsend[at] = normed
            else:
                kv1[at, pl.ds(0, 32)] = normed
        for copy in odd_copies(g):
            copy.start()

    for g in range(groups + 1):
        if g < groups:
            pair_copy(g).wait_recv()
            attend(0, kv0, g, put0)
            for half in range(2):
                feed(0, mix0, half, g)
                halo_copy(0, half, g).start()
        if g >= 1:
            for side in range(2):
                halo_copy(0, side, g - 1).wait_recv()
            multiply0(g - 1)
        if g >= 2:
            add0(g - 2)
            send_odd(g - 2)
    add0(groups - 1)
    send_odd(groups - 1)
    pad_weights(1)

    def put1(n, mixed):
        mix1[1, n] = mixed[0:32]
        ret[n] = mixed[32:64]

    def step1(g, carry):
        for copy in odd_copies(g):
            copy.wait_recv()
        attend(1, kv1, g, put1)
        ret_copy(g).start()
        feed(1, mix1, 1, g)
        return carry

    def step2(g, carry):
        ret_copy(g).wait_recv()
        feed(1, mix1, 0, g)
        return carry

    lax.fori_loop(0, groups, step1, 0)
    halo_copy(1, 1).start()

    def finish1(r):
        row = convolve(1, r, cols - HALF, cols - HALF - 1)
        row = pltpu.roll(row.T, HALF, 1)
        xs[pl.ds(r, channels, stride=rows), :] = row[0:channels]

    for r in range(HALF + 1, rows - 1):
        finish1(r)
    lax.fori_loop(0, groups, step2, 0)
    halo_copy(1, 0).start()
    for r in range(1, HALF + 1):
        finish1(r)
    for side in range(2):
        halo_copy(1, side).wait_recv()
    finish1(0)
    finish1(rows - 1)
    out[0] = xs[...].reshape(channels, rows, cols).astype(BF16)

    for g in range(groups):
        pair_copy(g).wait_send()
        for copy in odd_copies(g):
            copy.wait_send()
        ret_copy(g).wait_send()
        for side in range(2):
            halo_copy(0, side, g).wait_send()
    for side in range(2):
        halo_copy(1, side).wait_send()


def on_device(*args):
    frames = args[0]
    _, channels, rows, cols = frames.shape
    windows = cols // WIN
    groups = windows // GROUP
    dma = pltpu.SemaphoreType.DMA
    vmem = pl.BlockSpec(memory_space=pltpu.VMEM)
    return pl.pallas_call(
        kernel,
        out_shape=jax.ShapeDtypeStruct(frames.shape, BF16),
        in_specs=[pl.BlockSpec(memory_space=pltpu.HBM)] * len(args),
        out_specs=vmem,
        scratch_shapes=[pltpu.VMEM(arg.shape, arg.dtype) for arg in args]
        + [
            dma((len(args),)),
            pltpu.VMEM((channels * rows, cols), F32),
            pltpu.VMEM((2, windows, HALF, WIN, LANES), F32),
            pltpu.VMEM((rows, cols + 8, LANES), F32),
            pltpu.VMEM((rows, cols + 8, 384), F32),
            pltpu.VMEM((windows, 128, LANES), BF16),
            pltpu.VMEM((windows, 128, LANES), BF16),
            pltpu.VMEM((windows, 32, LANES), BF16),
            pltpu.VMEM((windows, 32, LANES), BF16),
            pltpu.VMEM((2, windows, 32, LANES), BF16),
            pltpu.VMEM((2, windows, 32, LANES), BF16),
            pltpu.VMEM((rows + 2, cols, LANES), BF16),
            pltpu.VMEM((rows + 2, cols, LANES), BF16),
            pltpu.VMEM((LAYERS, LANES, 384), BF16),
            pltpu.VMEM((LAYERS, LANES, LANES), BF16),
            pltpu.VMEM((LAYERS, LANES, 512), BF16),
            pltpu.VMEM((LAYERS, 256, LANES), BF16),
            pltpu.VMEM((LAYERS, 384, 384), BF16),
            pltpu.VMEM((256, 384), F32),
            pltpu.VMEM((8, LANES), F32),
            dma((groups,)), dma((groups,)),
            dma((3, groups)), dma((3, groups)),
            dma((groups,)), dma((groups,)),
            dma((groups + 1, 2)), dma((groups + 1, 2)),
        ],
        compiler_params=pltpu.CompilerParams(
            collective_id=0, has_side_effects=True, vmem_limit_bytes=63 * 2**20
        ),
    )(*args)


def solution(mesh):
    in_specs = (P(("clips", "tm"), None, "tile", None), P(), P(), P(), P(), P(), P(), P(), P())
    out_specs = P(("clips", "tm"), None, "tile", None)
    return jax.shard_map(
        on_device, mesh=mesh, in_specs=in_specs, out_specs=out_specs, check_vma=False
    )
```
